512 devices in a mesh: fsdp: 64 (over z_lo, y, core), rep: 8 (over z_hi, x).
Axes of the slice: x: 4, y: 8, z: 8 (z_hi: 2, z_lo: 4; z = z_hi * 4 + z_lo), core: 2. Of those that a mesh axis runs over, the one named last changes fastest.
Arguments:
- patches: bfloat16 [131072, 2048], P(('fsdp', 'rep')), may hold values from -24 to 24
- cotangent: bfloat16 [131072, 2048], P(('fsdp', 'rep')), may hold values from -0.015625 to 0.015625
- student: float32 [2048, 2048], P('fsdp'), may hold values from -6 to 6
- first_moment: float32 [2048, 2048], P('fsdp'), may hold values from -4 to 4
- second_moment: float32 [2048, 2048], P('fsdp'), may hold values from 0.0005 to 0.03
- teacher: float32 [2048, 2048], P('fsdp'), may hold values from -6 to 6
Outputs:
- features: bfloat16 [131072, 2048], P(('fsdp', 'rep'))
- new_student: float32 [2048, 2048], P('fsdp')
- new_first: float32 [2048, 2048], P('fsdp')
- new_second: float32 [2048, 2048], P('fsdp')
- new_teacher: float32 [2048, 2048], P('fsdp')
The draws below stay inside these ranges and needn't reach their ends.
All inputs are finite; a program needn't handle non-finite values.
Results may differ from the reference program's by a relative error of at most 0.006.
Values may be sent and summed in bfloat16 or wider, within the bound.
A program may use at most 128 MiB of HBM per device.

```python
import math
import jax
import jax.numpy as jnp
from jax import lax

FEAT = 2048
OUTW = 2048
TOK_DEV = 256
STEP = 100
TOKENS = 131072
N_FSDP = 64
N_REP = 8


def with_spikes(result, key, source, target, parts, factor):
    def block_of(axis_at):
        return (jnp.arange(result.shape[axis_at]) // (result.shape[axis_at] // parts)).reshape((-1,) + (1,) * (result.ndim - 1 - axis_at))

    one_side = jax.random.permutation(key, parts)[block_of(target)]
    second = (block_of(target) + parts // 2) % parts
    return jnp.where((block_of(source) == one_side) | (block_of(source) == second), factor * result, result)


def steps_of(key, dims, cuts, smallest, largest):
    def one(dim, parts):
        steps = jax.random.uniform(jax.random.fold_in(jax.random.fold_in(key, 6), dim), (parts,), jnp.float32, smallest / len(cuts), largest / len(cuts))
        return jnp.repeat(jnp.exp(steps), dims[dim] // parts).reshape((-1,) + (1,) * (len(dims) - dim - 1))

    gain = one(*cuts[0])
    for cut in cuts[1:]:
        gain = gain * one(*cut)
    return gain


def scatter_about(own_key, extent, scale, bound, pieces=(), kind=jnp.bfloat16):
    values = scale * jax.random.normal(own_key, extent, jnp.float32)
    if pieces:
        values = values * steps_of(own_key, extent, pieces, -0.22, 0.18)
    return jnp.clip(values, -bound, bound).astype(kind)


def noise_with(own_key, shape, width, limit, shards, heavy, dtype=jnp.bfloat16):
    array = width * jax.random.normal(own_key, shape, jnp.float32)
    if shards:
        array = array * steps_of(own_key, shape, shards, -0.22, 0.18)
    return jnp.clip(with_spikes(array, jax.random.fold_in(own_key, 3), *heavy), -limit, limit).astype(dtype)


def setup_inputs(seed: int = 0) -> dict:
    streams_of = jax.random.split(jax.random.key(seed), 7)
    patches = noise_with(streams_of[0], (TOKENS, FEAT), 1.0, 24.0, ((0, 512),), (0, 1, 512, 6.0))
    cotangent = scatter_about(streams_of[1], (TOKENS, OUTW), TOKENS ** -0.5, 0.015625, ((0, 512),))
    student = scatter_about(streams_of[2], (FEAT, OUTW), 1.0, 6.0, ((0, 64),), jnp.float32)
    first_moment = scatter_about(streams_of[3], (FEAT, OUTW), 0.3, 4.0, ((0, 64),), jnp.float32)
    second_moment = jnp.clip(jnp.exp(math.log(0.03) - 4.0943445 * jax.random.uniform(streams_of[4], (FEAT, OUTW), jnp.float32) ** steps_of(streams_of[4], (FEAT, OUTW), ((0, 64),), -0.2, 0.2)), 0.0005, 0.03)
    teacher = scatter_about(streams_of[5], (FEAT, OUTW), 1.0, 6.0, ((0, 64),), jnp.float32)
    return {"patches": patches, "cotangent": cotangent, "student": student, "first_moment": first_moment, "second_moment": second_moment, "teacher": teacher}


beta_one = 0.9
beta_two = 0.999
adam_eps = 1e-08
learn_rate = 0.1
decay_rate = 0.04
ema_keep = 0.994

def reference(patches, cotangent, student, first_moment, second_moment, teacher):
    teacher_weights = teacher.astype(jnp.bfloat16)
    features = (jnp.dot(patches, teacher_weights, preferred_element_type=jnp.float32) * FEAT ** (-0.5)).astype(jnp.bfloat16)
    device_count = N_FSDP * N_REP
    split_patches = patches.reshape(device_count, TOK_DEV, FEAT)
    split_cotangent = cotangent.reshape(device_count, TOK_DEV, OUTW)

    def add_term(total, pair):
        term = jnp.dot(pair[0].T, pair[1], preferred_element_type=jnp.float32).astype(jnp.bfloat16)
        return (total + term.astype(jnp.float32), None)
    gradient, unused = lax.scan(add_term, jnp.zeros((FEAT, OUTW), jnp.float32), (split_patches, split_cotangent))
    new_first = beta_one * first_moment + (1.0 - beta_one) * gradient
    new_second = beta_two * second_moment + (1.0 - beta_two) * gradient * gradient
    corr_one = 1.0 - beta_one ** STEP
    corr_two = 1.0 - beta_two ** STEP
    direction = new_first / corr_one / (jnp.sqrt(new_second / corr_two) + adam_eps)
    new_student = student - learn_rate * (direction + decay_rate * student)
    new_teacher = ema_keep * teacher + (1.0 - ema_keep) * new_student
    return (features, new_student, new_first, new_second, new_teacher)
```

```python
import jax
import jax.numpy as jnp
from jax import lax
from jax.experimental import pallas as pl
from jax.experimental.pallas import tpu as pltpu
from jax.sharding import PartitionSpec as P

FEAT = 2048
STEP = 100

beta_one = 0.9
beta_two = 0.999
adam_eps = 1e-08
learn_rate = 0.1
decay_rate = 0.04
ema_keep = 0.994

NX, NY, NL, NH = 4, 8, 4, 2
NZ = NL * NH
TOK = 256
HALF = 1024
WA = 384
WB = HALF - WA
XW = 512
MESH = pl.DeviceIdType.MESH
N_SEND = 160
N_RECV = 128
BF = jnp.bfloat16
F32 = jnp.float32


def update_shard(gradient, student, first_moment, second_moment, teacher):
    new_first = beta_one * first_moment + (1.0 - beta_one) * gradient
    new_second = beta_two * second_moment + (1.0 - beta_two) * gradient * gradient
    corr_one = 1.0 - beta_one**STEP
    corr_two = 1.0 - beta_two**STEP
    direction = new_first / corr_one / (jnp.sqrt(new_second / corr_two) + adam_eps)
    new_student = student - learn_rate * (direction + decay_rate * student)
    new_teacher = ema_keep * teacher + (1.0 - ema_keep) * new_student
    return (new_student, new_first, new_second, new_teacher)


def kernel(
    p_ref, c_ref, t_ref,
    feat_ref, grad_ref,
    w, pt, cc, buf_a, buf_b, sum_a, sum_b, got_a, got_b, four_a, four_b, piece, whole,
    send_sem, recv_sem,
):
    fs = lax.axis_index("fsdp")
    rp = lax.axis_index("rep")
    core = lax.rem(fs, 2)
    y = lax.rem(fs // 2, NY)
    zl = fs // (2 * NY)
    zh = rp // NX
    x = lax.rem(rp, NX)
    z = zh * NL + zl
    other = 1 - core

    def dev(x_, y_, z_, c_):
        return ((lax.rem(z_, NL) * NY + y_) * 2 + c_, (z_ // NL) * NX + x_)

    def at_x(d):
        return dev(lax.rem(x + d + NX, NX), y, z, core)

    def at_y(d):
        return dev(x, lax.rem(y + d + NY, NY), z, core)

    def at_z(d):
        return dev(x, y, lax.rem(z + d + NZ, NZ), core)

    sister = dev(x, y, z, other)
    counts = {"s": 0, "r": 0}
    sent = []

    def new_recv():
        counts["r"] += 1
        return counts["r"] - 1

    def send(src, dst, r, to):
        s = counts["s"]
        counts["s"] += 1
        cp = pltpu.make_async_remote_copy(
            src_ref=src, dst_ref=dst, send_sem=send_sem.at[s], recv_sem=recv_sem.at[r],
            device_id=to, device_id_type=MESH,
        )
        cp.start()
        sent.append(cp)

    def wait(dst, r):
        pltpu.make_async_remote_copy(
            src_ref=dst, dst_ref=dst, send_sem=send_sem.at[0], recv_sem=recv_sem.at[r],
            device_id=sister, device_id_type=MESH,
        ).wait_recv()

    barrier = pltpu.get_barrier_semaphore()
    partners = [sister]
    partners += [at_y(d) for d in range(1, NY)]
    partners += [at_z(d) for d in range(1, NZ)]
    partners += [at_x(d) for d in range(1, NX)]
    partners += [dev(x, y, lax.rem(z + NL, NZ), other)]
    for to in partners:
        pl.semaphore_signal(barrier, inc=1, device_id=to, device_id_type=MESH)

    def wblock(xx, yy, cr, lo=0, n=NL):
        return w.at[xx, pl.ds(lo, n), yy, cr]

    def wone(xx, ll, yy, cr):
        return w.at[xx, ll, yy, cr]

    wone(x, zl, y, core)[...] = t_ref[:, pl.ds(pl.multiple_of(x * XW, XW), XW)].astype(BF)
    my_tok = pl.ds(pl.multiple_of(core * TOK, TOK), TOK)
    ot_tok = pl.ds(pl.multiple_of(other * TOK, TOK), TOK)
    for j in range(8):
        pt[j // 2, pl.ds((j % 2) * 4, 4), :, my_tok] = (
            p_ref[:, j * 256:(j + 1) * 256].T.reshape(4, 64, TOK)
        )
    cc[my_tok, :] = c_ref[:, pl.ds(pl.multiple_of(core * HALF, HALF), HALF)]

    pl.semaphore_wait(barrier, len(partners))

    r_c, r_p = new_recv(), new_recv()
    send(c_ref.at[:, pl.ds(pl.multiple_of(other * HALF, HALF), HALF)], cc.at[my_tok, :], r_c, sister)
    send(pt.at[:, :, :, my_tok], pt.at[:, :, :, my_tok], r_p, sister)

    r_z = [new_recv() for _ in range(3)]
    for r, d in zip(r_z, (1, -1, 2)):
        send(wone(x, zl, y, core), wone(x, zl, y, core), r, at_z(d))
    for r, d in zip(r_z, (1, -1, 2)):
        wait(wone(x, lax.rem(zl - d + NL, NL), y, core), r)

    r_sis = [new_recv() for _ in range(NX)]
    r_xr = [new_recv() for _ in range(NY)]
    r_xl = [new_recv() for _ in range(NY)]
    r_opp = [new_recv() for _ in range(NY)]
    r_yr = [new_recv() for _ in range(4)]
    r_yl = [new_recv() for _ in range(4)]
    offs = [0, -1, 1, -2, 2, -3, 3, 4]
    ys = [lax.rem(y + o + NY, NY) for o in offs]
    xs = [x, lax.rem(x - 1 + NX, NX), lax.rem(x + 1, NX), lax.rem(x + 2, NX)]

    def to_sister(k, j):
        send(wblock(xs[k], ys[j], core), wblock(xs[k], ys[j], core), r_sis[k], sister)

    def fan(j):
        b = wblock(x, ys[j], core)
        send(b, b, r_xr[j], at_x(1))
        send(b, b, r_xl[j], at_x(-1))
        to_sister(0, j)

    def y_own():
        b = wblock(x, y, core)
        send(b, b, r_yr[0], at_y(1))
        send(b, b, r_yl[0], at_y(-1))
        fan(0)

    def y_arrive(k):
        if k < 4:
            for o, rs, d, lo in ((-k, r_yr, 1, 0), (k, r_yl, -1, 2)):
                yy = lax.rem(y + o + NY, NY)
                wait(wblock(x, yy, core), rs[k - 1])
                b = wblock(x, yy, core) if k < 3 else wblock(x, yy, core, lo, 2)
                send(b, b, rs[k], at_y(d))
                fan(2 * k - 1 if o < 0 else 2 * k)
        else:
            yy = lax.rem(y + 4, NY)
            wait(wblock(x, yy, core, 0, 2), r_yr[3])
            wait(wblock(x, yy, core, 2, 2), r_yl[3])
            fan(7)

    def x_arrive(j):
        b = wblock(xs[1], ys[j], core)
        wait(b, r_xr[j])
        if j % 2 == 0:
            send(b, b, r_opp[j], at_x(1))
        to_sister(1, j)
        b = wblock(xs[2], ys[j], core)
        wait(b, r_xl[j])
        if j % 2 == 1:
            send(b, b, r_opp[j], at_x(-1))
        to_sister(2, j)

    def opp_arrive(j):
        wait(wblock(xs[3], ys[j], core), r_opp[j])
        to_sister(3, j)

    def features(k):
        xx = xs[k]
        wait(w.at[xx, :, :, other], r_sis[k])
        total = jnp.zeros((TOK, XW), F32)
        for ll in range(NL):
            total += jnp.dot(
                p_ref[:, ll * 512:(ll + 1) * 512],
                w[xx, ll].reshape(512, XW),
                preferred_element_type=F32,
            )
        feat_ref[:, pl.ds(pl.multiple_of(xx * XW, XW), XW)] = (total * FEAT ** (-0.5)).astype(BF)

    def term_a(q, h):
        rows = pt[pl.ds(2 * h, 2), q].reshape(128, 2 * TOK)
        return jnp.dot(rows, cc[:, :WA], preferred_element_type=F32).reshape(2, 64, WA)

    def term_b(q, h):
        rows = pt[
            lax.rem(q, NL), pl.ds(4 * h, 4), pl.ds(pl.multiple_of((q // NL) * 32, 32), 32), :
        ].reshape(128, 2 * TOK)
        return jnp.dot(rows, cc[:, WA:], preferred_element_type=F32).reshape(4, 32, WB)

    streams = [(1, 0, 4), (-1, 1, 4), (1, 1, 3), (-1, 0, 3)]
    slot = {}
    n_slots = 0
    for d, h, length in streams:
        for t in range(length + 1):
            slot[(d, h, t)] = n_slots
            n_slots += 1
    r_ring = {}
    for part in "ab":
        for d, h, length in streams:
            for t in range(1, length + 1):
                r_ring[(part, d, h, t)] = new_recv()

    def ring_step(part, t):
        buf, term, pos, near = (
            (buf_a, term_a, y, at_y) if part == "a" else (buf_b, term_b, z, at_z)
        )
        for d, h, length in streams:
            if t > length:
                continue
            q = lax.rem(pos + d * (length + 1 - t) + 8, 8)
            here = slot[(d, h, t - 1)]
            value = term(q, h)
            if t > 1:
                wait(buf.at[here], r_ring[(part, d, h, t - 1)])
                value = value + buf[here].astype(F32)
            buf[here] = value.astype(BF)
            send(buf.at[here], buf.at[slot[(d, h, t)]], r_ring[(part, d, h, t)], near(d))

    def ring_end(part):
        buf, term, pos = (buf_a, term_a, y) if part == "a" else (buf_b, term_b, z)
        for h in range(2):
            value = term(pos, h)
            for d, hh, length in streams:
                if hh == h:
                    last = slot[(d, h, length)]
                    wait(buf.at[last], r_ring[(part, d, h, length)])
                    value = value + buf[last].astype(F32)
            if part == "a":
                sum_a[pl.ds(2 * h, 2)] = value.reshape(2, NH, 32, WA).astype(BF)
            else:
                sum_b[pl.ds(4 * h, 4)] = value.astype(BF)

    r_da, r_db = new_recv(), new_recv()
    r_xa = [new_recv() for _ in range(3)]
    r_xb = [new_recv() for _ in range(3)]

    def direct_a():
        for d in range(1, NZ):
            zz = lax.rem(z + d, NZ)
            send(sum_a.at[lax.rem(zz, NL), zz // NL], got_a.at[d - 1], r_da, at_z(d))

    def direct_b():
        for d in range(1, NY):
            send(sum_b.at[lax.rem(y + d, NY)], got_b.at[d - 1], r_db, at_y(d))

    def across(part):
        got, four, rd, rx = (
            (got_a, four_a, r_da, r_xa) if part == "a" else (got_b, four_b, r_db, r_xb)
        )
        wait(got, rd)
        value = (sum_a[zl, zh] if part == "a" else sum_b[y]).astype(F32)
        for k in range(7):
            value = value + got[k].astype(F32)
        four[x] = value.astype(BF)
        for d in range(1, NX):
            send(four.at[x], four.at[x], rx[d - 1], at_x(d))

    def finish(part):
        four, rx = (four_a, r_xa) if part == "a" else (four_b, r_xb)
        for d in range(1, NX):
            wait(four.at[lax.rem(x - d + NX, NX)], rx[d - 1])
        value = four[0].astype(F32)
        for k in range(1, NX):
            value = value + four[k].astype(F32)
        if part == "a":
            piece[:, :WA] = value.astype(BF)
        else:
            piece[:, WA:] = value.astype(BF)

    r_far, r_near = new_recv(), new_recv()

    def quad_send():
        send(piece, whole.at[core], r_far, dev(x, y, lax.rem(z + NL, NZ), zh))
        s = counts["s"]
        counts["s"] += 1

        @pl.when(core == zh)
        def _():
            whole[core] = piece[...]

        @pl.when(core != zh)
        def _():
            cp = pltpu.make_async_remote_copy(
                src_ref=piece, dst_ref=whole.at[core], send_sem=send_sem.at[s],
                recv_sem=recv_sem.at[r_near], device_id=sister, device_id_type=MESH,
            )
            cp.start()
            cp.wait_send()

    y_own()
    wait(cc.at[ot_tok, :], r_c)
    wait(pt.at[:, :, :, ot_tok], r_p)
    ring_step("a", 1)
    ring_step("b", 1)
    y_arrive(1)
    y_arrive(2)
    ring_step("a", 2)
    x_arrive(0)
    y_arrive(3)
    ring_step("b", 2)
    y_arrive(4)
    x_arrive(1)
    ring_step("a", 3)
    x_arrive(2)
    ring_step("b", 3)
    ring_step("a", 4)
    x_arrive(3)
    ring_step("b", 4)
    ring_end("a")
    direct_a()
    x_arrive(4)
    opp_arrive(0)
    opp_arrive(1)
    features(0)
    ring_end("b")
    direct_b()
    across("a")
    x_arrive(5)
    opp_arrive(2)
    opp_arrive(3)
    across("b")
    finish("a")
    x_arrive(6)
    opp_arrive(4)
    finish("b")
    quad_send()
    x_arrive(7)
    opp_arrive(5)
    features(1)
    features(2)
    opp_arrive(6)
    opp_arrive(7)

    @pl.when(zh == core)
    def _():
        wait(whole.at[other], r_near)

    @pl.when(zh != core)
    def _():
        wait(whole, r_far)

    grad_ref[:, :HALF] = whole[0]
    grad_ref[:, HALF:] = whole[1]
    features(3)
    for cp in sent:
        cp.wait_send()


def per_device(patches, cotangent, student, first_moment, second_moment, teacher):
    vmem = pl.BlockSpec(memory_space=pltpu.VMEM)
    features, gradient = pl.pallas_call(
        kernel,
        out_shape=(
            jax.ShapeDtypeStruct((TOK, FEAT), BF),
            jax.ShapeDtypeStruct((32, FEAT), BF),
        ),
        in_specs=[vmem] * 3,
        out_specs=(vmem, vmem),
        scratch_shapes=[
            pltpu.VMEM((NX, NL, NY, 2, 32, XW), BF),
            pltpu.VMEM((NL, NY, 64, 2 * TOK), BF),
            pltpu.VMEM((2 * TOK, HALF), BF),
            pltpu.VMEM((18, 2, 64, WA), BF),
            pltpu.VMEM((18, 4, 32, WB), BF),
            pltpu.VMEM((NL, NH, 32, WA), BF),
            pltpu.VMEM((NY, 32, WB), BF),
            pltpu.VMEM((7, 32, WA), BF),
            pltpu.VMEM((7, 32, WB), BF),
            pltpu.VMEM((NX, 32, WA), BF),
            pltpu.VMEM((NX, 32, WB), BF),
            pltpu.VMEM((32, HALF), BF),
            pltpu.VMEM((2, 32, HALF), BF),
            pltpu.SemaphoreType.DMA((N_SEND,)),
            pltpu.SemaphoreType.DMA((N_RECV,)),
        ],
        compiler_params=pltpu.CompilerParams(
            collective_id=0, has_side_effects=True, vmem_limit_bytes=56 * 2**20
        ),
    )(patches, cotangent, teacher)
    new_student, new_first, new_second, new_teacher = update_shard(
        gradient.astype(F32), student, first_moment, second_moment, teacher
    )
    return (features, new_student, new_first, new_second, new_teacher)


def solution(mesh):
    both = P(("fsdp", "rep"), None)
    rows = P("fsdp", None)
    return jax.shard_map(
        per_device,
        mesh=mesh,
        in_specs=(both, both, rows, rows, rows, rows),
        out_specs=(both, rows, rows, rows, rows),
        check_vma=False,
    )
```

```python
import jax
import jax.numpy as jnp
from jax import lax
from jax.experimental import pallas as pl
from jax.experimental.pallas import tpu as pltpu
from jax.sharding import PartitionSpec as P

FEAT = 2048
STEP = 100

beta_one = 0.9
beta_two = 0.999
adam_eps = 1e-08
learn_rate = 0.1
decay_rate = 0.04
ema_keep = 0.994

NX, NY, NL, NH = 4, 8, 4, 2
NZ = NL * NH
TOK = 256
HALF = 1024
WA = 512
WB = HALF - WA
XW = 512
MESH = pl.DeviceIdType.MESH
N_SEND = 160
N_RECV = 128
BF = jnp.bfloat16
F32 = jnp.float32


def update_shard(gradient, student, first_moment, second_moment, teacher):
    new_first = beta_one * first_moment + (1.0 - beta_one) * gradient
    new_second = beta_two * second_moment + (1.0 - beta_two) * gradient * gradient
    corr_one = 1.0 - beta_one**STEP
    corr_two = 1.0 - beta_two**STEP
    direction = new_first / corr_one / (jnp.sqrt(new_second / corr_two) + adam_eps)
    new_student = student - learn_rate * (direction + decay_rate * student)
    new_teacher = ema_keep * teacher + (1.0 - ema_keep) * new_student
    return (new_student, new_first, new_second, new_teacher)


def kernel(
    p_ref, c_ref, t_ref,
    feat_ref, grad_ref,
    p_v, t_v, feat_v, w, pt, cc, buf_a, buf_b, sum_a, sum_b, got_a, got_b, four_a, four_b, piece_a, piece_b, whole_a, whole_b,
    load_sem, send_sem, recv_sem,
):
    fs = lax.axis_index("fsdp")
    rp = lax.axis_index("rep")
    core = lax.rem(fs, 2)
    y = lax.rem(fs // 2, NY)
    zl = fs // (2 * NY)
    zh = rp // NX
    x = lax.rem(rp, NX)
    z = zh * NL + zl
    other = 1 - core

    def dev(x_, y_, z_, c_):
        return ((lax.rem(z_, NL) * NY + y_) * 2 + c_, (z_ // NL) * NX + x_)

    def at_x(d):
        return dev(lax.rem(x + d + NX, NX), y, z, core)

    def at_y(d):
        return dev(x, lax.rem(y + d + NY, NY), z, core)

    def at_z(d):
        return dev(x, y, lax.rem(z + d + NZ, NZ), core)

    sister = dev(x, y, z, other)
    counts = {"s": 0, "r": 0}
    sent = []

    def new_recv():
        counts["r"] += 1
        return counts["r"] - 1

    def send(src, dst, r, to):
        s = counts["s"]
        counts["s"] += 1
        cp = pltpu.make_async_remote_copy(
            src_ref=src, dst_ref=dst, send_sem=send_sem.at[s], recv_sem=recv_sem.at[r],
            device_id=to, device_id_type=MESH,
        )
        cp.start()
        sent.append(cp)

    def wait(dst, r):
        pltpu.make_async_remote_copy(
            src_ref=dst, dst_ref=dst, send_sem=send_sem.at[0], recv_sem=recv_sem.at[r],
            device_id=sister, device_id_type=MESH,
        ).wait_recv()

    barrier = pltpu.get_barrier_semaphore()
    partners = [sister]
    partners += [at_y(d) for d in range(1, NY)]
    partners += [at_z(d) for d in range(1, NZ)]
    partners += [at_x(d) for d in range(1, NX)]
    partners += [dev(x, y, lax.rem(z + NL, NZ), other)]
    for to in partners:
        pl.semaphore_signal(barrier, inc=1, device_id=to, device_id_type=MESH)

    def wblock(xx, yy, cr, lo=0, n=NL):
        return w.at[xx, pl.ds(lo, n), yy, cr]

    def wone(xx, ll, yy, cr):
        return w.at[xx, ll, yy, cr]

    my_tok = pl.ds(pl.multiple_of(core * TOK, TOK), TOK)
    ot_tok = pl.ds(pl.multiple_of(other * TOK, TOK), TOK)
    loads = [
        pltpu.make_async_copy(
            t_ref.at[:, pl.ds(pl.multiple_of(x * XW, XW), XW)], t_v, load_sem.at[0]
        ),
        pltpu.make_async_copy(p_ref, p_v, load_sem.at[1]),
        pltpu.make_async_copy(
            c_ref.at[:, pl.ds(pl.multiple_of(core * HALF, HALF), HALF)],
            cc.at[my_tok, :], load_sem.at[2],
        ),
    ]
    for cp in loads:
        cp.start()
    loads[0].wait()
    wone(x, zl, y, core)[...] = t_v[...].astype(BF)
    loads[1].wait()

    def turn(ll):
        for j in (2 * ll, 2 * ll + 1):
            pt[ll, pl.ds((j % 2) * 4, 4), :, my_tok] = (
                p_v[:, j * 256:(j + 1) * 256].T.reshape(4, 64, TOK)
            )

    turn(0)
    pl.semaphore_wait(barrier, len(partners))

    r_c = new_recv()
    r_p = [new_recv() for _ in range(NL)]
    r_z = [new_recv() for _ in range(3)]
    for r, d in zip(r_z, (1, -1, 2)):
        send(wone(x, zl, y, core), wone(x, zl, y, core), r, at_z(d))
    send(c_ref.at[:, pl.ds(pl.multiple_of(other * HALF, HALF), HALF)], cc.at[my_tok, :], r_c, sister)
    for ll in range(NL):
        if ll:
            turn(ll)
        send(pt.at[ll, :, :, my_tok], pt.at[ll, :, :, my_tok], r_p[ll], sister)
    loads[2].wait()

    for r, d in zip(r_z, (1, -1, 2)):
        wait(wone(x, lax.rem(zl - d + NL, NL), y, core), r)

    r_sis = [new_recv() for _ in range(NX)]
    r_xr = [new_recv() for _ in range(NY)]
    r_xl = [new_recv() for _ in range(NY)]
    r_opp = [new_recv() for _ in range(NY)]
    r_yr = [new_recv() for _ in range(4)]
    r_yl = [new_recv() for _ in range(4)]
    offs = [0, -1, 1, -2, 2, -3, 3, 4]
    ys = [lax.rem(y + o + NY, NY) for o in offs]
    xs = [x, lax.rem(x - 1 + NX, NX), lax.rem(x + 1, NX), lax.rem(x + 2, NX)]

    def to_sister(k, j):
        send(wblock(xs[k], ys[j], core), wblock(xs[k], ys[j], core), r_sis[k], sister)

    def fan(j):
        b = wblock(x, ys[j], core)
        send(b, b, r_xr[j], at_x(1))
        send(b, b, r_xl[j], at_x(-1))
        to_sister(0, j)

    def y_own():
        b = wblock(x, y, core)
        send(b, b, r_yr[0], at_y(1))
        send(b, b, r_yl[0], at_y(-1))
        fan(0)

    def y_from(side, k):
        o, rs, d, lo = ((-k, r_yr, 1, 0), (k, r_yl, -1, 2))[side]
        yy = lax.rem(y + o + NY, NY)
        wait(wblock(x, yy, core), rs[k - 1])
        b = wblock(x, yy, core) if k < 3 else wblock(x, yy, core, lo, 2)
        send(b, b, rs[k], at_y(d))
        fan(2 * k - 1 if o < 0 else 2 * k)

    def y_last():
        yy = lax.rem(y + 4, NY)
        wait(wblock(x, yy, core, 0, 2), r_yr[3])
        wait(wblock(x, yy, core, 2, 2), r_yl[3])
        fan(7)

    def x_from(side, j):
        rs, d = ((r_xr, 1), (r_xl, -1))[side]
        b = wblock(xs[1 + side], ys[j], core)
        wait(b, rs[j])
        if j % 2 == side:
            send(b, b, r_opp[j], at_x(d))
        to_sister(1 + side, j)

    def opp_arrive(j):
        wait(wblock(xs[3], ys[j], core), r_opp[j])
        to_sister(3, j)

    def features(k):
        xx = xs[k]
        wait(w.at[xx, :, :, other], r_sis[k])
        total = jnp.zeros((TOK, XW), F32)
        for ll in range(NL):
            total += jnp.dot(
                p_v[:, ll * 512:(ll + 1) * 512],
                w[xx, ll].reshape(512, XW),
                preferred_element_type=F32,
            )
        feat_v[k] = (total * FEAT ** (-0.5)).astype(BF)
        feat_copy(k).start()

    def feat_copy(k):
        cols = pl.ds(pl.multiple_of(xs[k] * XW, XW), XW)
        return pltpu.make_async_copy(feat_v.at[k], feat_ref.at[:, cols], load_sem.at[3 + k])

    def term_a(q, h):
        rows = pt[pl.ds(2 * h, 2), q].reshape(128, 2 * TOK)
        return jnp.dot(rows, cc[:, :WA], preferred_element_type=F32).reshape(2, 64, WA)

    def term_b(q, h):
        rows = pt[
            lax.rem(q, NL), pl.ds(4 * h, 4), pl.ds(pl.multiple_of((q // NL) * 32, 32), 32), :
        ].reshape(128, 2 * TOK)
        return jnp.dot(rows, cc[:, WA:], preferred_element_type=F32).reshape(4, 32, WB)

    streams = [(1, 0, 4), (-1, 1, 4), (1, 1, 3), (-1, 0, 3)]
    slot = {}
    n_slots = 0
    for d, h, length in streams:
        for t in range(length + 1):
            slot[(d, h, t)] = n_slots
            n_slots += 1
    r_ring = {}
    for part in "ab":
        for d, h, length in streams:
            for t in range(1, length + 1):
                r_ring[(part, d, h, t)] = new_recv()

    def ring_step(part, i, t):
        buf, term, pos, near = (
            (buf_a, term_a, y, at_y) if part == "a" else (buf_b, term_b, z, at_z)
        )
        d, h, length = streams[i]
        q = lax.rem(pos + d * (length + 1 - t) + 8, 8)
        here = slot[(d, h, t - 1)]
        value = term(q, h)
        if t > 1:
            wait(buf.at[here], r_ring[(part, d, h, t - 1)])
            value = value + buf[here].astype(F32)
        buf[here] = value.astype(BF)
        send(buf.at[here], buf.at[slot[(d, h, t)]], r_ring[(part, d, h, t)], near(d))

    def ring_end(part, h):
        buf, term, pos = (buf_a, term_a, y) if part == "a" else (buf_b, term_b, z)
        value = term(pos, h)
        for d, hh, length in streams:
            if hh == h:
                last = slot[(d, h, length)]
                wait(buf.at[last], r_ring[(part, d, h, length)])
                value = value + buf[last].astype(F32)
        if part == "a":
            sum_a[pl.ds(2 * h, 2)] = value.reshape(2, NH, 32, WA).astype(BF)
        else:
            sum_b[pl.ds(4 * h, 4)] = value.astype(BF)

    r_da, r_db = new_recv(), new_recv()
    def direct_a():
        for d in range(1, NZ):
            zz = lax.rem(z + d, NZ)
            send(sum_a.at[lax.rem(zz, NL), zz // NL], got_a.at[d - 1], r_da, at_z(d))

    def direct_b():
        for d in range(1, NY):
            send(sum_b.at[lax.rem(y + d, NY)], got_b.at[d - 1], r_db, at_y(d))

    r_x = {part: [new_recv() for _ in range(3)] for part in "ab"}
    r_far = {part: new_recv() for part in "ab"}
    r_near = {part: new_recv() for part in "ab"}

    def across(part):
        got, four, rd = (got_a, four_a, r_da) if part == "a" else (got_b, four_b, r_db)
        wait(got, rd)
        value = (sum_a[zl, zh] if part == "a" else sum_b[y]).astype(F32)
        for k in range(7):
            value = value + got[k].astype(F32)
        four[x] = value.astype(BF)
        for d in range(1, NX):
            send(four.at[x], four.at[x], r_x[part][d - 1], at_x(d))

    def quad(part):
        four, piece, whole = (four_a, piece_a, whole_a) if part == "a" else (four_b, piece_b, whole_b)
        for d in range(1, NX):
            wait(four.at[lax.rem(x - d + NX, NX)], r_x[part][d - 1])
        value = four[0].astype(F32)
        for k in range(1, NX):
            value = value + four[k].astype(F32)
        piece[...] = value.astype(BF)
        send(piece, whole.at[core], r_far[part], dev(x, y, lax.rem(z + NL, NZ), zh))
        s = counts["s"]
        counts["s"] += 1

        @pl.when(core == zh)
        def _():
            whole[core] = piece[...]

        @pl.when(core != zh)
        def _():
            cp = pltpu.make_async_remote_copy(
                src_ref=piece, dst_ref=whole.at[core], send_sem=send_sem.at[s],
                recv_sem=recv_sem.at[r_near[part]], device_id=sister, device_id_type=MESH,
            )
            cp.start()
            cp.wait_send()

    def collect(part):
        whole, lo, n = (whole_a, 0, WA) if part == "a" else (whole_b, WA, WB)

        @pl.when(zh == core)
        def _():
            wait(whole.at[other], r_near[part])

        @pl.when(zh != core)
        def _():
            wait(whole, r_far[part])

        for cr in range(2):
            grad_ref[:, cr * HALF + lo:cr * HALF + lo + n] = whole[cr]

    y_own()
    wait(cc.at[ot_tok, :], r_c)
    for ll in range(NL):
        wait(pt.at[ll, :, :, ot_tok], r_p[ll])
    ring_step("a", 0, 1)
    ring_step("a", 1, 1)
    ring_step("b", 1, 1)
    y_from(0, 1)
    ring_step("b", 0, 1)
    ring_step("a", 3, 1)
    ring_step("b", 3, 1)
    ring_step("b", 2, 1)
    ring_step("a", 0, 2)
    y_from(1, 1)
    ring_step("b", 1, 2)
    ring_step("b", 0, 2)
    ring_step("a", 1, 2)
    y_from(0, 2)
    ring_step("a", 2, 1)
    ring_step("b", 2, 2)
    ring_step("b", 3, 2)
    ring_step("a", 0, 3)
    y_from(1, 2)
    ring_step("b", 1, 3)
    ring_step("b", 0, 3)
    y_from(0, 3)
    x_from(0, 2)
    x_from(0, 3)
    ring_step("a", 3, 2)
    x_from(1, 1)
    ring_step("a", 2, 2)
    ring_step("b", 2, 3)
    x_from(0, 0)
    x_from(1, 2)
    ring_step("a", 1, 3)
    ring_step("b", 3, 3)
    ring_step("b", 0, 4)
    ring_step("a", 3, 3)
    ring_step("a", 0, 4)
    ring_step("b", 1, 4)
    ring_step("a", 1, 4)
    x_from(1, 3)
    opp_arrive(2)
    ring_step("a", 2, 3)
    y_from(1, 3)
    x_from(0, 4)
    ring_end("b", 0)
    ring_end("b", 1)
    direct_b()
    ring_end("a", 0)
    ring_end("a", 1)
    direct_a()
    x_from(1, 5)
    x_from(0, 1)
    y_last()
    x_from(0, 6)
    features(0)
    x_from(1, 6)
    x_from(1, 4)
    across("b")
    opp_arrive(1)
    x_from(0, 5)
    x_from(0, 7)
    across("a")
    x_from(1, 7)
    opp_arrive(0)
    quad("b")
    opp_arrive(6)
    opp_arrive(5)
    features(1)
    quad("a")
    opp_arrive(3)
    x_from(1, 0)
    opp_arrive(4)
    opp_arrive(7)
    features(2)
    features(3)
    collect("b")
    collect("a")
    for k in range(NX):
        feat_copy(k).wait()
    for cp in sent:
        cp.wait_send()


def per_device(patches, cotangent, student, first_moment, second_moment, teacher):
    vmem = pl.BlockSpec(memory_space=pltpu.VMEM)
    hbm = pl.BlockSpec(memory_space=pl.ANY)
    features, gradient = pl.pallas_call(
        kernel,
        out_shape=(
            jax.ShapeDtypeStruct((TOK, FEAT), BF),
            jax.ShapeDtypeStruct((32, FEAT), BF),
        ),
        in_specs=[hbm] * 3,
        out_specs=(hbm, vmem),
        scratch_shapes=[
            pltpu.VMEM((TOK, FEAT), BF),
            pltpu.VMEM((32, XW), F32),
            pltpu.VMEM((NX, TOK, XW), BF),
            pltpu.VMEM((NX, NL, NY, 2, 32, XW), BF),
            pltpu.VMEM((NL, NY, 64, 2 * TOK), BF),
            pltpu.VMEM((2 * TOK, HALF), BF),
            pltpu.VMEM((18, 2, 64, WA), BF),
            pltpu.VMEM((18, 4, 32, WB), BF),
            pltpu.VMEM((NL, NH, 32, WA), BF),
            pltpu.VMEM((NY, 32, WB), BF),
            pltpu.VMEM((7, 32, WA), BF),
            pltpu.VMEM((7, 32, WB), BF),
            pltpu.VMEM((NX, 32, WA), BF),
            pltpu.VMEM((NX, 32, WB), BF),
            pltpu.VMEM((32, WA), BF),
            pltpu.VMEM((32, WB), BF),
            pltpu.VMEM((2, 32, WA), BF),
            pltpu.VMEM((2, 32, WB), BF),
            pltpu.SemaphoreType.DMA((3 + NX,)),
            pltpu.SemaphoreType.DMA((N_SEND,)),
            pltpu.SemaphoreType.DMA((N_RECV,)),
        ],
        compiler_params=pltpu.CompilerParams(
            collective_id=0, has_side_effects=True, vmem_limit_bytes=56 * 2**20
        ),
    )(patches, cotangent, teacher)
    new_student, new_first, new_second, new_teacher = update_shard(
        gradient.astype(F32), student, first_moment, second_moment, teacher
    )
    return (features, new_student, new_first, new_second, new_teacher)


def solution(mesh):
    both = P(("fsdp", "rep"), None)
    rows = P("fsdp", None)
    return jax.shard_map(
        per_device,
        mesh=mesh,
        in_specs=(both, both, rows, rows, rows, rows),
        out_specs=(both, rows, rows, rows, rows),
        check_vma=False,
    )
```

```python
import jax
import jax.numpy as jnp
from jax import lax
from jax.experimental import pallas as pl
from jax.experimental.pallas import tpu as pltpu
from jax.sharding import PartitionSpec as P

FEAT = 2048
STEP = 100

beta_one = 0.9
beta_two = 0.999
adam_eps = 1e-08
learn_rate = 0.1
decay_rate = 0.04
ema_keep = 0.994

NX, NY, NL, NH = 4, 8, 4, 2
NZ = NL * NH
TOK = 256
HALF = 1024
WA = 512
WB = HALF - WA
XW = 512
MESH = pl.DeviceIdType.MESH
N_SEND = 160
N_RECV = 128
BF = jnp.bfloat16
F32 = jnp.float32


def update_shard(gradient, student, first_moment, second_moment, teacher):
    new_first = beta_one * first_moment + (1.0 - beta_one) * gradient
    new_second = beta_two * second_moment + (1.0 - beta_two) * gradient * gradient
    corr_one = 1.0 - beta_one**STEP
    corr_two = 1.0 - beta_two**STEP
    direction = new_first / corr_one / (jnp.sqrt(new_second / corr_two) + adam_eps)
    new_student = student - learn_rate * (direction + decay_rate * student)
    new_teacher = ema_keep * teacher + (1.0 - ema_keep) * new_student
    return (new_student, new_first, new_second, new_teacher)


def kernel(
    p_ref, c_ref, t_ref,
    feat_ref, grad_ref,
    p_v, t_v, feat_v, w, pt, cc, buf_a, buf_b, sum_a, sum_b, got_a, got_b, four_a, four_b, piece_a, piece_b, whole_a, whole_b,
    load_sem, send_sem, recv_sem,
):
    fs = lax.axis_index("fsdp")
    rp = lax.axis_index("rep")
    core = lax.rem(fs, 2)
    y = lax.rem(fs // 2, NY)
    zl = fs // (2 * NY)
    zh = rp // NX
    x = lax.rem(rp, NX)
    z = zh * NL + zl
    other = 1 - core

    def dev(x_, y_, z_, c_):
        return ((lax.rem(z_, NL) * NY + y_) * 2 + c_, (z_ // NL) * NX + x_)

    def at_x(d):
        return dev(lax.rem(x + d + NX, NX), y, z, core)

    def at_y(d):
        return dev(x, lax.rem(y + d + NY, NY), z, core)

    def at_z(d):
        return dev(x, y, lax.rem(z + d + NZ, NZ), core)

    sister = dev(x, y, z, other)
    counts = {"s": 0, "r": 0}
    sent = []

    def new_recv():
        counts["r"] += 1
        return counts["r"] - 1

    def send(src, dst, r, to):
        s = counts["s"]
        counts["s"] += 1
        cp = pltpu.make_async_remote_copy(
            src_ref=src, dst_ref=dst, send_sem=send_sem.at[s], recv_sem=recv_sem.at[r],
            device_id=to, device_id_type=MESH,
        )
        cp.start()
        sent.append(cp)

    def wait(dst, r):
        pltpu.make_async_remote_copy(
            src_ref=dst, dst_ref=dst, send_sem=send_sem.at[0], recv_sem=recv_sem.at[r],
            device_id=sister, device_id_type=MESH,
        ).wait_recv()

    barrier = pltpu.get_barrier_semaphore()
    partners = [sister]
    partners += [at_y(d) for d in range(1, NY)]
    partners += [at_z(d) for d in range(1, NZ)]
    partners += [at_x(d) for d in range(1, NX)]
    partners += [dev(x, y, lax.rem(z + NL, NZ), other)]
    for to in partners:
        pl.semaphore_signal(barrier, inc=1, device_id=to, device_id_type=MESH)

    def wblock(xx, yy, cr, lo=0, n=NL):
        return w.at[xx, pl.ds(lo, n), yy, cr]

    def wone(xx, ll, yy, cr):
        return w.at[xx, ll, yy, cr]

    my_tok = pl.ds(pl.multiple_of(core * TOK, TOK), TOK)
    ot_tok = pl.ds(pl.multiple_of(other * TOK, TOK), TOK)
    loads = [
        pltpu.make_async_copy(
            t_ref.at[:, pl.ds(pl.multiple_of(x * XW, XW), XW)], t_v, load_sem.at[0]
        ),
        pltpu.make_async_copy(p_ref, p_v, load_sem.at[1]),
        pltpu.make_async_copy(
            c_ref.at[:, pl.ds(pl.multiple_of(core * HALF, HALF), HALF)],
            cc.at[my_tok, :], load_sem.at[2],
        ),
    ]
    for cp in loads:
        cp.start()
    loads[0].wait()
    wone(x, zl, y, core)[...] = t_v[...].astype(BF)

    def turn(ll):
        for j in range(2):
            cols = pl.ds(pl.multiple_of(ll * 512 + j * 256, 256), 256)
            pt[ll, pl.ds(j * 4, 4), :, my_tok] = p_v[:, cols].T.reshape(4, 64, TOK)

    pl.semaphore_wait(barrier, len(partners))

    r_c = new_recv()
    r_p = [new_recv() for _ in range(NL)]
    r_z = [new_recv() for _ in range(3)]
    for r, d in zip(r_z, (1, -1, 2)):
        send(wone(x, zl, y, core), wone(x, zl, y, core), r, at_z(d))
    send(c_ref.at[:, pl.ds(pl.multiple_of(other * HALF, HALF), HALF)], cc.at[my_tok, :], r_c, sister)
    groups = [lax.rem(zl + k, NL) for k in (0, 1, 3, 2)]
    loads[1].wait()
    for k, ll in enumerate(groups):
        turn(ll)
        send(pt.at[ll, :, :, my_tok], pt.at[ll, :, :, my_tok], r_p[k], sister)
    loads[2].wait()

    for r, d in zip(r_z, (1, -1, 2)):
        wait(wone(x, lax.rem(zl - d + NL, NL), y, core), r)

    r_sis = [new_recv() for _ in range(NX)]
    r_xr = [new_recv() for _ in range(NY)]
    r_xl = [new_recv() for _ in range(NY)]
    r_opp = [new_recv() for _ in range(NY)]
    r_yr = [new_recv() for _ in range(4)]
    r_yl = [new_recv() for _ in range(4)]
    offs = [0, -1, 1, -2, 2, -3, 3, 4]
    ys = [lax.rem(y + o + NY, NY) for o in offs]
    xs = [x, lax.rem(x - 1 + NX, NX), lax.rem(x + 1, NX), lax.rem(x + 2, NX)]

    def to_sister(k, j):
        send(wblock(xs[k], ys[j], core), wblock(xs[k], ys[j], core), r_sis[k], sister)

    def fan(j):
        b = wblock(x, ys[j], core)
        send(b, b, r_xr[j], at_x(1))
        send(b, b, r_xl[j], at_x(-1))
        to_sister(0, j)

    def y_own():
        b = wblock(x, y, core)
        send(b, b, r_yr[0], at_y(1))
        send(b, b, r_yl[0], at_y(-1))
        fan(0)

    def y_from(side, k):
        o, rs, d, lo = ((-k, r_yr, 1, 0), (k, r_yl, -1, 2))[side]
        yy = lax.rem(y + o + NY, NY)
        wait(wblock(x, yy, core), rs[k - 1])
        b = wblock(x, yy, core) if k < 3 else wblock(x, yy, core, lo, 2)
        send(b, b, rs[k], at_y(d))
        fan(2 * k - 1 if o < 0 else 2 * k)

    def y_last():
        yy = lax.rem(y + 4, NY)
        wait(wblock(x, yy, core, 0, 2), r_yr[3])
        wait(wblock(x, yy, core, 2, 2), r_yl[3])
        fan(7)

    def x_from(side, j):
        rs, d = ((r_xr, 1), (r_xl, -1))[side]
        b = wblock(xs[1 + side], ys[j], core)
        wait(b, rs[j])
        if j % 2 == side:
            send(b, b, r_opp[j], at_x(d))
        to_sister(1 + side, j)

    def opp_arrive(j):
        wait(wblock(xs[3], ys[j], core), r_opp[j])
        to_sister(3, j)

    def features(k):
        xx = xs[k]
        wait(w.at[xx, :, :, other], r_sis[k])
        total = jnp.zeros((TOK, XW), F32)
        for ll in range(NL):
            total += jnp.dot(
                p_v[:, ll * 512:(ll + 1) * 512],
                w[xx, ll].reshape(512, XW),
                preferred_element_type=F32,
            )
        feat_v[k] = (total * FEAT ** (-0.5)).astype(BF)
        feat_copy(k).start()

    def feat_copy(k):
        cols = pl.ds(pl.multiple_of(xs[k] * XW, XW), XW)
        return pltpu.make_async_copy(feat_v.at[k], feat_ref.at[:, cols], load_sem.at[3 + k])

    def term_a(q, h):
        rows = pt[pl.ds(2 * h, 2), q].reshape(128, 2 * TOK)
        return jnp.dot(rows, cc[:, :WA], preferred_element_type=F32).reshape(2, 64, WA)

    def term_b(q, h):
        rows = pt[
            lax.rem(q, NL), pl.ds(4 * h, 4), pl.ds(pl.multiple_of((q // NL) * 32, 32), 32), :
        ].reshape(128, 2 * TOK)
        return jnp.dot(rows, cc[:, WA:], preferred_element_type=F32).reshape(4, 32, WB)

    streams = [(1, 0, 4), (-1, 1, 4), (1, 1, 3), (-1, 0, 3)]
    slot = {}
    n_slots = 0
    for d, h, length in streams:
        for t in range(length + 1):
            slot[(d, h, t)] = n_slots
            n_slots += 1
    r_ring = {}
    for part in "ab":
        for d, h, length in streams:
            for t in range(1, length + 1):
                r_ring[(part, d, h, t)] = new_recv()

    def ring_step(part, i, t):
        buf, term, pos, near = (
            (buf_a, term_a, y, at_y) if part == "a" else (buf_b, term_b, z, at_z)
        )
        d, h, length = streams[i]
        q = lax.rem(pos + d * (length + 1 - t) + 8, 8)
        here = slot[(d, h, t - 1)]
        value = term(q, h)
        if t > 1:
            wait(buf.at[here], r_ring[(part, d, h, t - 1)])
            value = value + buf[here].astype(F32)
        buf[here] = value.astype(BF)
        send(buf.at[here], buf.at[slot[(d, h, t)]], r_ring[(part, d, h, t)], near(d))

    def ring_end(part, h):
        buf, term, pos = (buf_a, term_a, y) if part == "a" else (buf_b, term_b, z)
        value = term(pos, h)
        for d, hh, length in streams:
            if hh == h:
                last = slot[(d, h, length)]
                wait(buf.at[last], r_ring[(part, d, h, length)])
                value = value + buf[last].astype(F32)
        if part == "a":
            sum_a[pl.ds(2 * h, 2)] = value.reshape(2, NH, 32, WA).astype(BF)
        else:
            sum_b[pl.ds(4 * h, 4)] = value.astype(BF)

    r_da, r_db = new_recv(), new_recv()
    def direct_a():
        for d in (4, 3, 5, 2, 6, 1, 7):
            zz = lax.rem(z + d, NZ)
            send(sum_a.at[lax.rem(zz, NL), zz // NL], got_a.at[d - 1], r_da, at_z(d))

    def direct_b():
        for d in (4, 3, 5, 2, 6, 1, 7):
            send(sum_b.at[lax.rem(y + d, NY)], got_b.at[d - 1], r_db, at_y(d))

    r_x = {part: [new_recv() for _ in range(3)] for part in "ab"}
    r_far = {part: new_recv() for part in "ab"}
    r_near = {part: new_recv() for part in "ab"}

    def across(part):
        got, four, rd = (got_a, four_a, r_da) if part == "a" else (got_b, four_b, r_db)
        wait(got, rd)
        value = (sum_a[zl, zh] if part == "a" else sum_b[y]).astype(F32)
        for k in range(7):
            value = value + got[k].astype(F32)
        four[x] = value.astype(BF)
        for d in (2, 1, 3):
            send(four.at[x], four.at[x], r_x[part][d - 1], at_x(d))

    def quad(part):
        four, piece, whole = (four_a, piece_a, whole_a) if part == "a" else (four_b, piece_b, whole_b)
        for d in range(1, NX):
            wait(four.at[lax.rem(x - d + NX, NX)], r_x[part][d - 1])
        value = four[0].astype(F32)
        for k in range(1, NX):
            value = value + four[k].astype(F32)
        piece[...] = value.astype(BF)
        send(piece, whole.at[core], r_far[part], dev(x, y, lax.rem(z + NL, NZ), zh))
        s = counts["s"]
        counts["s"] += 1

        @pl.when(core == zh)
        def _():
            whole[core] = piece[...]

        @pl.when(core != zh)
        def _():
            cp = pltpu.make_async_remote_copy(
                src_ref=piece, dst_ref=whole.at[core], send_sem=send_sem.at[s],
                recv_sem=recv_sem.at[r_near[part]], device_id=sister, device_id_type=MESH,
            )
            cp.start()
            cp.wait_send()

    def collect(part):
        whole, lo, n = (whole_a, 0, WA) if part == "a" else (whole_b, WA, WB)

        @pl.when(zh == core)
        def _():
            wait(whole.at[other], r_near[part])

        @pl.when(zh != core)
        def _():
            wait(whole, r_far[part])

        for cr in range(2):
            grad_ref[:, cr * HALF + lo:cr * HALF + lo + n] = whole[cr]

    y_own()
    wait(cc.at[ot_tok, :], r_c)
    wait(pt.at[groups[0], :, :, ot_tok], r_p[0])
    ring_step("b", 0, 1)
    ring_step("b", 1, 1)
    wait(pt.at[groups[1], :, :, ot_tok], r_p[1])
    ring_step("b", 3, 1)
    wait(pt.at[groups[2], :, :, ot_tok], r_p[2])
    ring_step("b", 2, 1)
    wait(pt.at[groups[3], :, :, ot_tok], r_p[3])
    ring_step("a", 0, 1)
    ring_step("a", 1, 1)
    y_from(0, 1)
    ring_step("a", 3, 1)
    ring_step("a", 0, 2)
    y_from(1, 1)
    ring_step("b", 1, 2)
    ring_step("b", 0, 2)
    ring_step("a", 1, 2)
    y_from(0, 2)
    ring_step("a", 2, 1)
    ring_step("b", 2, 2)
    ring_step("b", 3, 2)
    ring_step("a", 0, 3)
    y_from(1, 2)
    ring_step("b", 1, 3)
    ring_step("b", 0, 3)
    y_from(0, 3)
    x_from(0, 2)
    x_from(0, 3)
    ring_step("a", 3, 2)
    x_from(1, 1)
    ring_step("a", 2, 2)
    ring_step("b", 2, 3)
    x_from(0, 0)
    x_from(1, 2)
    ring_step("a", 1, 3)
    ring_step("b", 3, 3)
    ring_step("b", 0, 4)
    ring_step("a", 3, 3)
    ring_step("a", 0, 4)
    ring_step("b", 1, 4)
    ring_step("a", 1, 4)
    x_from(1, 3)
    opp_arrive(2)
    ring_step("a", 2, 3)
    y_from(1, 3)
    x_from(0, 4)
    ring_end("b", 0)
    ring_end("b", 1)
    direct_b()
    ring_end("a", 0)
    ring_end("a", 1)
    direct_a()
    x_from(1, 5)
    x_from(0, 1)
    y_last()
    x_from(0, 6)
    features(0)
    x_from(1, 6)
    x_from(1, 4)
    across("b")
    opp_arrive(1)
    x_from(0, 5)
    x_from(0, 7)
    across("a")
    x_from(1, 7)
    opp_arrive(0)
    quad("b")
    opp_arrive(6)
    opp_arrive(5)
    features(1)
    quad("a")
    opp_arrive(3)
    x_from(1, 0)
    opp_arrive(4)
    opp_arrive(7)
    features(2)
    features(3)
    collect("b")
    collect("a")
    for k in range(NX):
        feat_copy(k).wait()
    for cp in sent:
        cp.wait_send()


def per_device(patches, cotangent, student, first_moment, second_moment, teacher):
    vmem = pl.BlockSpec(memory_space=pltpu.VMEM)
    hbm = pl.BlockSpec(memory_space=pl.ANY)
    features, gradient = pl.pallas_call(
        kernel,
        out_shape=(
            jax.ShapeDtypeStruct((TOK, FEAT), BF),
            jax.ShapeDtypeStruct((32, FEAT), BF),
        ),
        in_specs=[hbm] * 3,
        out_specs=(hbm, vmem),
        scratch_shapes=[
            pltpu.VMEM((TOK, FEAT), BF),
            pltpu.VMEM((32, XW), F32),
            pltpu.VMEM((NX, TOK, XW), BF),
            pltpu.VMEM((NX, NL, NY, 2, 32, XW), BF),
            pltpu.VMEM((NL, NY, 64, 2 * TOK), BF),
            pltpu.VMEM((2 * TOK, HALF), BF),
            pltpu.VMEM((18, 2, 64, WA), BF),
            pltpu.VMEM((18, 4, 32, WB), BF),
            pltpu.VMEM((NL, NH, 32, WA), BF),
            pltpu.VMEM((NY, 32, WB), BF),
            pltpu.VMEM((7, 32, WA), BF),
            pltpu.VMEM((7, 32, WB), BF),
            pltpu.VMEM((NX, 32, WA), BF),
            pltpu.VMEM((NX, 32, WB), BF),
            pltpu.VMEM((32, WA), BF),
            pltpu.VMEM((32, WB), BF),
            pltpu.VMEM((2, 32, WA), BF),
            pltpu.VMEM((2, 32, WB), BF),
            pltpu.SemaphoreType.DMA((3 + NX,)),
            pltpu.SemaphoreType.DMA((N_SEND,)),
            pltpu.SemaphoreType.DMA((N_RECV,)),
        ],
        compiler_params=pltpu.CompilerParams(
            collective_id=0, has_side_effects=True, vmem_limit_bytes=56 * 2**20
        ),
    )(patches, cotangent, teacher)
    new_student, new_first, new_second, new_teacher = update_shard(
        gradient.astype(F32), student, first_moment, second_moment, teacher
    )
    return (features, new_student, new_first, new_second, new_teacher)


def solution(mesh):
    both = P(("fsdp", "rep"), None)
    rows = P("fsdp", None)
    return jax.shard_map(
        per_device,
        mesh=mesh,
        in_specs=(both, both, rows, rows, rows, rows),
        out_specs=(both, rows, rows, rows, rows),
        check_vma=False,
    )
```
